32 devices in a mesh: grp: 2 (over x), row: 16 (over z, y, core).
Axes of the slice: x: 2, y: 2, z: 4, core: 2. Of those that a mesh axis runs over, the one named last changes fastest.
Arguments:
- matrix: bfloat16 [32, 2048, 16384], P(('grp', 'row')), parts along dimension 0, may hold values from -1 to 1
- probes: bfloat16 [16384, 128], P(('grp', 'row')), parts along dimension 0, may hold values from -6 to 6
Outputs:
- basis_out: bfloat16 [16384, 128], P(('grp', 'row')), parts along dimension 0
- sketch_out: bfloat16 [32, 4096, 128], P(('grp', 'row')), parts along dimension 0
The draws below stay inside these ranges and needn't reach their ends.
There are 2 independent parts, one for each index of `grp`. The reference program is written for one: setup_inputs(seed, part) draws one part's arguments, and reference() takes and returns one part's arrays. A program takes and returns all parts, laid end to end along the dimension named above; each array names one. Nothing has to cross between parts.
All inputs are finite; a program needn't handle non-finite values.
Results may differ from the reference program's by a relative error of at most 0.012.
Values may be sent and summed in bfloat16 or wider, within the bound.
A program may use at most 192 MiB of HBM per device.

```python
import math
import jax
import jax.numpy as jnp
from jax import lax

VOCAB = 65536
PROBES = 128
GRID_ROWS = 4
TILE_ROWS = 2048
ITERS = 2
GRID_COLS = 4
TILE_COLS = 16384
M = 8192
SKETCH_ROWS = 4096
N_ROW = 16


def draw_matrix(key, part):
    first, second, third = jax.random.split(jax.random.fold_in(key, 7), 3)
    index = jnp.arange(M, dtype=jnp.float32)
    rising = jnp.exp(jnp.log(3.0) * index / (M - 1.0))[:, None]
    base = jnp.clip(jax.random.normal(first, (M, VOCAB), jnp.float32), -6.0, 6.0)
    spread = jnp.exp(jax.random.uniform(second, (M, 1), jnp.float32, jnp.log(0.8), jnp.log(1.25)))
    columns = jnp.exp(jax.random.uniform(third, (1, VOCAB), jnp.float32, jnp.log(0.6), jnp.log(1.6)))
    values = jnp.clip(base * rising * spread * columns / jnp.sqrt(jnp.float32(M)), -1.0, 1.0)
    tiles = values.reshape(GRID_ROWS, TILE_ROWS, GRID_COLS, TILE_COLS).transpose(0, 2, 1, 3)
    return tiles.reshape(GRID_ROWS * GRID_COLS, TILE_ROWS, TILE_COLS).astype(jnp.bfloat16)


def block_scale(key, extent, cuts, smallest, high):
    level = 1.0
    for axis_at, parts in cuts:
        heights = jax.random.uniform(jax.random.fold_in(jax.random.fold_in(key, 6), axis_at), (parts,), jnp.float32, smallest / len(cuts), high / len(cuts))
        level = level * jnp.repeat(jnp.exp(heights), extent[axis_at] // parts).reshape((-1,) + (1,) * (len(extent) - 1 - axis_at))
    return level


def centred(key, extent, deviation, reach, cuts=(), kind=jnp.bfloat16):
    drawn = jax.random.normal(key, extent, jnp.float32) * deviation
    if len(cuts) > 0:
        drawn = block_scale(key, extent, cuts, -0.22, 0.18) * drawn
    return jnp.clip(drawn, min=-reach, max=reach).astype(kind)


def setup_inputs(seed: int = 0, part: int = 0) -> dict:
    seeds = jax.random.split(jax.random.key(seed), 3)
    part_keys = jax.random.split(jax.random.fold_in(seeds[2], part), 3)
    matrix = draw_matrix(jax.random.fold_in(jax.random.fold_in(seeds[2], part), 71), part)
    probes = centred(part_keys[1], (M, PROBES), 1.0, 6.0, ((0, 16),))
    return {"matrix": matrix, "probes": probes}


def reference(matrix, probes):
    whole = matrix.reshape(GRID_ROWS, GRID_COLS, TILE_ROWS, TILE_COLS).transpose(0, 2, 1, 3).reshape(M, VOCAB)
    current = probes
    sketch = None
    for iteration in range(ITERS):
        sketch = lax.dot_general(whole.astype(jnp.float32), current.astype(jnp.float32), (((0,), (0,)), ((), ())), preferred_element_type=jnp.float32).astype(jnp.bfloat16)
        product = jnp.dot(whole.astype(jnp.float32), sketch.astype(jnp.float32), preferred_element_type=jnp.float32)
        gram_matrix = jnp.dot(product.T.astype(jnp.float32), product.astype(jnp.float32), precision=lax.Precision.HIGHEST, preferred_element_type=jnp.float32)
        factor = jnp.linalg.cholesky(gram_matrix)
        solved = lax.linalg.triangular_solve(factor, product, left_side=False, lower=True, transpose_a=True)
        current = (solved * math.sqrt(M)).astype(jnp.bfloat16)
    blocks = sketch.reshape(GRID_COLS, GRID_ROWS, SKETCH_ROWS, PROBES).transpose(1, 0, 2, 3).reshape(N_ROW, SKETCH_ROWS, PROBES)
    return (current, blocks)
```

```python
import functools
import math

import jax
import jax.numpy as jnp
from jax import lax
from jax.experimental import pallas as pl
from jax.experimental.pallas import tpu as pltpu
from jax.sharding import PartitionSpec as P

GRID_ROWS = 4
ITERS = 2
CHUNK = 512
LAG_MID, LAG_SUM, LAG_END = 2, 4, 6
AHEAD = 3
WINDOW = AHEAD + LAG_END
MESH = pl.DeviceIdType.MESH


def remote(src, dst, send_sem, recv_sem, target):
    return pltpu.make_async_remote_copy(
        src_ref=src, dst_ref=dst, send_sem=send_sem, recv_sem=recv_sem,
        device_id={"row": target}, device_id_type=MESH,
    )


def stage_kernel(
    cols, chunk, a_ref, cur_ref, image_ref, gram_ref, block_ref,
    a_buf, own, outgoing, landed, crossed, total, panel, panel_t, acc,
    share_out, share_in, gram_row, gram_col,
    a_sem, send_a, send_b, recv_a, recv_b,
    panel_send, panel_recv, share_send, share_recv,
    row_send, row_recv, col_send, col_recv,
):
    me = lax.axis_index("row")
    grid_row, col = me // cols, lax.rem(me, cols)
    base = grid_row * cols
    slab = cur_ref.shape[0]
    steps = a_ref.shape[1] // chunk
    is_end = (grid_row == 0) | (grid_row == GRID_ROWS - 1)
    is_mid = jnp.logical_not(is_end)
    neighbour = (grid_row ^ 1) * cols + col
    opposite = (GRID_ROWS - 1 - grid_row) * cols + col

    def row_peer(off):
        return lax.rem(col + off, cols)

    def col_peer(off):
        return lax.rem(grid_row + off, GRID_ROWS)

    def each(count, body):
        lax.fori_loop(1, count, lambda off, c: (body(off), c)[1], 0)

    def fetch(step):
        slot = lax.rem(step, WINDOW)
        return pltpu.make_async_copy(
            a_ref.at[:, pl.ds(pl.multiple_of(step * chunk, chunk), chunk)],
            a_buf.at[slot], a_sem.at[slot],
        )

    for step in range(min(AHEAD, steps)):
        fetch(step).start()

    barrier = pltpu.get_barrier_semaphore()

    def greet(target):
        pl.semaphore_signal(barrier, inc=1, device_id={"row": target}, device_id_type=MESH)

    each(cols, lambda off: greet(base + row_peer(off)))
    each(GRID_ROWS, lambda off: greet(col_peer(off) * cols + col))
    pl.semaphore_wait(barrier, cols - 1 + GRID_ROWS - 1)

    def slab_of(index):
        return pl.ds(pl.multiple_of(index * slab, slab), slab)

    def panel_copy(sender, target):
        return remote(
            cur_ref, panel.at[slab_of(sender)], panel_send.at[target], panel_recv.at[sender],
            base + target,
        )

    each(cols, lambda off: panel_copy(col, row_peer(off)).start())
    panel[slab_of(col), :] = cur_ref[...]
    acc[...] = jnp.zeros_like(acc)
    each(cols, lambda off: panel_copy(row_peer(off), row_peer(off)).wait_recv())
    panel_t[...] = panel[...].astype(jnp.float32).T.astype(jnp.bfloat16)

    def rows_of(step):
        return pl.ds(pl.multiple_of(step * chunk, chunk), chunk)

    def to_neighbour(source, sem, step):
        return remote(
            source.at[rows_of(step)], landed.at[rows_of(step)], sem.at[step], recv_a.at[step],
            neighbour,
        )

    def to_opposite(step):
        return remote(
            outgoing.at[rows_of(step)], crossed.at[rows_of(step)], send_a.at[step],
            recv_b.at[step], opposite,
        )

    def body(step, carry):
        @pl.when(step < steps)
        def _():
            fetch(step).wait()
            part = jnp.dot(
                panel_t[...], a_buf[lax.rem(step, WINDOW)], preferred_element_type=jnp.float32
            ).T

            @pl.when(is_end)
            def _():
                outgoing[rows_of(step), :] = part.astype(jnp.bfloat16)
                to_neighbour(outgoing, send_a, step).start()

            @pl.when(is_mid)
            def _():
                own[lax.rem(step, WINDOW)] = part

        mid = step - LAG_MID

        @pl.when(is_mid & (mid >= 0) & (mid < steps))
        def _():
            slot = lax.rem(mid, WINDOW)
            to_neighbour(total, send_b, mid).wait_recv()
            pair = own[slot] + landed[rows_of(mid), :].astype(jnp.float32)
            own[slot] = pair
            outgoing[rows_of(mid), :] = pair.astype(jnp.bfloat16)
            to_opposite(mid).start()

        last = step - jnp.where(is_end, LAG_END, LAG_SUM)

        @pl.when((last >= 0) & (last < steps))
        def _():
            slot = lax.rem(last, WINDOW)

            @pl.when(is_mid)
            def _():
                to_opposite(last).wait_recv()
                whole = own[slot] + crossed[rows_of(last), :].astype(jnp.float32)
                total[rows_of(last), :] = whole.astype(jnp.bfloat16)
                to_neighbour(total, send_b, last).start()

            @pl.when(is_end)
            def _():
                to_neighbour(outgoing, send_a, last).wait_recv()
                total[rows_of(last), :] = landed[rows_of(last), :]

            acc[...] += jnp.dot(
                a_buf[slot], total[rows_of(last), :], preferred_element_type=jnp.float32
            )

        @pl.when(step + AHEAD < steps)
        def _():
            fetch(step + AHEAD).start()

        return carry

    lax.fori_loop(0, steps + LAG_END, body, 0)

    def share_copy(sender, target):
        return remote(
            share_out.at[slab_of(target)], share_in.at[sender], share_send.at[target],
            share_recv.at[sender], base + target,
        )

    share_out[...] = acc[...].astype(jnp.bfloat16)
    each(cols, lambda off: share_copy(col, row_peer(off)).start())
    share = block_ref.shape[0]
    block_ref[...] = total[pl.ds(pl.multiple_of(grid_row * share, share), share), :]
    image_ref[...] = acc[slab_of(col), :]

    def add_share(off):
        sender = row_peer(off)
        share_copy(sender, sender).wait_recv()
        image_ref[...] += share_in[sender].astype(jnp.float32)

    each(cols, add_share)

    def row_copy(sender, target):
        return remote(
            gram_row.at[col], gram_row.at[sender], row_send.at[target], row_recv.at[sender],
            base + target,
        )

    def col_copy(sender, target):
        return remote(
            gram_col.at[grid_row], gram_col.at[sender], col_send.at[target], col_recv.at[sender],
            target * cols + col,
        )

    image = image_ref[...]
    gram_row[col] = jnp.dot(
        image.T, image, precision=lax.Precision.HIGHEST, preferred_element_type=jnp.float32
    )
    each(cols, lambda off: row_copy(col, row_peer(off)).start())
    each(cols, lambda off: row_copy(row_peer(off), row_peer(off)).wait_recv())
    row_sum = lax.fori_loop(
        1, cols, lambda i, value: value + gram_row[i], gram_row[0]
    )
    gram_col[grid_row] = row_sum
    each(GRID_ROWS, lambda off: col_copy(grid_row, col_peer(off)).start())
    each(GRID_ROWS, lambda off: col_copy(col_peer(off), col_peer(off)).wait_recv())
    gram_ref[...] = (gram_col[0] + gram_col[1]) + (gram_col[2] + gram_col[3])

    each(cols, lambda off: panel_copy(col, row_peer(off)).wait_send())
    each(cols, lambda off: share_copy(col, row_peer(off)).wait_send())
    each(cols, lambda off: row_copy(col, row_peer(off)).wait_send())
    each(GRID_ROWS, lambda off: col_copy(grid_row, col_peer(off)).wait_send())

    def drain(step, carry):
        to_opposite(step).wait_send()

        @pl.when(is_mid)
        def _():
            to_neighbour(total, send_b, step).wait_send()

        return carry

    lax.fori_loop(0, steps, drain, 0)


def stage(tile, current, cols):
    rows, words = tile.shape
    slab, probes = current.shape
    chunk = min(CHUNK, words)
    steps = words // chunk
    half, full = jnp.bfloat16, jnp.float32
    sems = [
        (WINDOW,), (steps,), (steps,), (steps,), (steps,),
        (cols,), (cols,), (cols,), (cols,), (cols,), (cols,), (GRID_ROWS,), (GRID_ROWS,),
    ]
    vmem = pl.BlockSpec(memory_space=pltpu.VMEM)
    return pl.pallas_call(
        functools.partial(stage_kernel, cols, chunk),
        out_shape=(
            jax.ShapeDtypeStruct((slab, probes), full),
            jax.ShapeDtypeStruct((probes, probes), full),
            jax.ShapeDtypeStruct((words // GRID_ROWS, probes), half),
        ),
        in_specs=[pl.BlockSpec(memory_space=pl.ANY), vmem],
        out_specs=(vmem, vmem, vmem),
        scratch_shapes=[
            pltpu.VMEM((WINDOW, rows, chunk), half),
            pltpu.VMEM((WINDOW, chunk, probes), full),
            pltpu.VMEM((words, probes), half),
            pltpu.VMEM((words, probes), half),
            pltpu.VMEM((words, probes), half),
            pltpu.VMEM((words, probes), half),
            pltpu.VMEM((rows, probes), half),
            pltpu.VMEM((probes, rows), half),
            pltpu.VMEM((rows, probes), full),
            pltpu.VMEM((rows, probes), half),
            pltpu.VMEM((cols, slab, probes), half),
            pltpu.VMEM((cols, probes, probes), full),
            pltpu.VMEM((GRID_ROWS, probes, probes), full),
        ] + [pltpu.SemaphoreType.DMA(shape) for shape in sems],
        compiler_params=pltpu.CompilerParams(
            collective_id=0, has_side_effects=True, vmem_limit_bytes=56 * 2**20
        ),
        cost_estimate=pl.CostEstimate(
            flops=4 * rows * words * probes, bytes_accessed=2 * rows * words, transcendentals=0
        ),
    )(tile, current)


def orthonormal(product, gram_matrix, rescale):
    factor = jnp.linalg.cholesky(gram_matrix)
    solved = lax.linalg.triangular_solve(
        factor, product, left_side=False, lower=True, transpose_a=True
    )
    return (solved * rescale).astype(jnp.bfloat16)


def per_device(matrix, probes):
    tile = matrix[0]
    cols = lax.axis_size("row") // GRID_ROWS
    rescale = math.sqrt(GRID_ROWS * tile.shape[0])
    current, block = probes, None
    for _ in range(ITERS):
        image, gram_matrix, block = stage(tile, current, cols)
        current = orthonormal(image, gram_matrix, rescale)
    return (current, block[None])


def solution(mesh):
    placed = (P(("grp", "row"), None, None), P(("grp", "row"), None))
    return jax.shard_map(
        per_device,
        mesh=mesh,
        in_specs=placed,
        out_specs=(P(("grp", "row"), None), P(("grp", "row"), None, None)),
        check_vma=False,
    )
```
